32 devices in a mesh: dp: 2 (over core), expert: 4 (over y, x), mp: 4 (over z).
Axes of the slice: x: 2, y: 2, z: 4, core: 2. Of those that a mesh axis runs over, the one named last changes fastest.
Arguments:
- hidden_in: bfloat16 [4096, 2048], P(('dp', 'expert')), may hold values from -6 to 6
- norm_gain: float32 [2048], replicated, may hold values from 0.1 to 1.9
- router_w: bfloat16 [2048, 4], replicated, may hold values from -0.0625 to 0.0625
- choices: int32 [4096, 2], P(('dp', 'expert')), may hold values from 0 to 3, all different within a row; in each aligned block of 512 rows (0 to 511, 512 to 1023, ...) at most 384 rows name the same one
- w_gate: bfloat16 [4, 2048, 5632], P('expert', None, 'mp'), may hold values from -0.125 to 0.125
- w_up: bfloat16 [4, 2048, 5632], P('expert', None, 'mp'), may hold values from -0.125 to 0.125
- w_down: bfloat16 [4, 5632, 2048], P('expert', 'mp'), may hold values from -0.109375 to 0.109375
Outputs:
- block_out: bfloat16 [4096, 2048], P(('dp', 'expert'), 'mp')
The draws below stay inside these ranges and needn't reach their ends.
Inputs may be any that keep to these rules, and one draw needn't show every extreme that they name: `choices`: each row names two different experts. Among the 512 rows of one block of tokens no expert is named more than 384 times, and in every draw some expert is named exactly 384 times in some block.
All inputs are finite; a program needn't handle non-finite values.
Results may differ from the reference program's by a relative error of at most 0.012.
Values may be sent and summed in bfloat16 or wider, within the bound.
A program may use at most 128 MiB of HBM per device.

```python
import math
import jax
import jax.numpy as jnp
import numpy as np
from jax import lax

D = 2048
FF = 5632
TOK_DEV = 512
E = 4
CAP = 384
TOKENS = 4096
N_DP = 2
N_EXPERT = 4
N_MP = 4


def spiked(array, rng, source, target, shards_of, factor):
    def block_of(dim):
        return (jnp.arange(array.shape[dim]) // (array.shape[dim] // shards_of)).reshape((-1,) + (1,) * (array.ndim - 1 - dim))

    one_side = jax.random.permutation(rng, shards_of)[block_of(target)]
    other_side = (block_of(target) + shards_of // 2) % shards_of
    return jnp.where((block_of(source) == one_side) | (block_of(source) == other_side), factor * array, array)


def steps_of(rng, dims, shards, least, high):
    def one(axis_at, blocks):
        heights = jax.random.uniform(jax.random.fold_in(jax.random.fold_in(rng, 6), axis_at), (blocks,), jnp.float32, least / len(shards), high / len(shards))
        return jnp.repeat(jnp.exp(heights), dims[axis_at] // blocks).reshape((-1,) + (1,) * (len(dims) - axis_at - 1))

    gain = one(*shards[0])
    for cut in shards[1:]:
        gain = gain * one(*cut)
    return gain


def shared_out(rng, own, number, rows, count, top, most, lean):
    ranking = jax.random.permutation(rng, count)
    heavy_load, usual = portions_of(count, rows * top, most, lean, True), portions_of(count, rows * top, most, lean, False)
    places = jnp.arange(count)

    def named(sizes, rotation):
        used = int((sizes > 0).sum())
        fixed = max(1, used // 4)
        passed = fixed + (places - fixed + rotation * (used - fixed)) % max(1, count - fixed)
        return jnp.zeros((count,), jnp.int32).at[ranking[jnp.where(places < fixed, places, passed)]].set(jnp.asarray(sizes, jnp.int32))

    sizes = jnp.where(number % 4 == 0, named(heavy_load, number // 4), named(usual, number - number // 4 - 1))
    mixed = jax.random.permutation(jax.random.fold_in(own, 3), count)
    donor, receiver = mixed[0:count // 2 * 2:2], mixed[1:count // 2 * 2:2]
    margin = jnp.minimum(sizes[donor] - 1, most - sizes[receiver]) // 2
    margin = jnp.where((donor == ranking[0]) | (receiver == ranking[0]) | (sizes[receiver] == 0), 0, jnp.maximum(margin, 0))
    passed = jax.random.randint(jax.random.fold_in(own, 4), (count // 2,), 0, 1 << 20) % (margin + 1)
    sizes = sizes.at[donor].add(-passed).at[receiver].add(passed)
    labels = jnp.searchsorted(jnp.cumsum(sizes), jnp.arange(rows * top), side="right").astype(jnp.int32)
    grid = labels.reshape(top, rows).T
    grid = grid[jax.random.permutation(jax.random.fold_in(own, 1), rows)]
    rotation = jax.random.randint(jax.random.fold_in(own, 2), (rows, 1), 0, top)
    return jnp.take_along_axis(grid, (jnp.arange(top)[None, :] + rotation) % top, axis=1)


def portions_of(count, total, limit, skew, full):
    weights = [(1 << 20) // math.isqrt(standing ** skew) + 1 for standing in range(1, count + 1)]
    largest = limit if full else min(limit, max(-(-total // count), total * weights[0] // sum(weights)))
    least = 1 if total - largest >= count - 1 else 0
    given, rest = [largest] + [least] * (count - 1), total - largest - least * (count - 1)
    while rest > 0:
        candidates = [i for i in range(1, count) if given[i] < largest] or [i for i in range(1, count) if given[i] < limit]
        whole, budget = sum([weights[i] for i in candidates]), rest
        for i in candidates:
            addition = min(limit - given[i], max(1, budget * weights[i] // whole), rest)
            given[i] = given[i] + addition
            rest = rest - addition
    return np.array(given)


def bell_draw(rng, shape, scale, most, cuts=(), kind=jnp.bfloat16):
    loudness = steps_of(rng, shape, cuts, -0.22, 0.18) if cuts else 1.0
    entries = jax.random.normal(rng, shape, jnp.float32) * scale * loudness
    return jnp.minimum(jnp.maximum(entries, -most), most).astype(kind)


def heavy_noise(stream_key, dims, width, most, split, heavy, held_as=jnp.bfloat16):
    array = width * jax.random.normal(stream_key, dims, jnp.float32)
    if split:
        array = array * steps_of(stream_key, dims, split, -0.22, 0.18)
    return jnp.clip(spiked(array, jax.random.fold_in(stream_key, 3), *heavy), -most, most).astype(held_as)


def setup_inputs(seed: int = 0) -> dict:
    key_list = jax.random.split(jax.random.key(seed), 8)
    hidden_in = bell_draw(key_list[0], (TOKENS, D), 1.0, 6.0, ((0, 8),))
    norm_gain = jnp.clip(1.0 + 0.18 * jax.random.normal(key_list[1], (D,), jnp.float32), 0.1, 1.9)
    router_w = bell_draw(key_list[2], (D, E), (D * 4) ** -0.5, 0.0625)
    choices_keys = jax.random.split(jax.random.fold_in(key_list[3], 1), TOKENS // TOK_DEV)
    choices_turns = jax.random.permutation(jax.random.fold_in(key_list[3], 3), TOKENS // TOK_DEV)
    choices = jax.vmap(lambda own, number: shared_out(jax.random.fold_in(key_list[3], 2), own, number, TOK_DEV, E, 2, CAP, 2))(choices_keys, choices_turns).reshape((TOKENS, 2))
    w_gate = bell_draw(key_list[4], (E, D, FF), D ** -0.5, 0.125, ((0, 4), (2, 4)))
    w_up = bell_draw(key_list[5], (E, D, FF), D ** -0.5, 0.125, ((0, 4), (2, 4)))
    w_down = heavy_noise(key_list[6], (E, FF, D), FF ** -0.5, 0.109375, ((0, 4), (1, 4)), (1, 2, 4, 2.0))
    return dict(hidden_in=hidden_in, norm_gain=norm_gain, router_w=router_w, choices=choices, w_gate=w_gate, w_up=w_up, w_down=w_down)


eps_norm = 1e-06

def pair_slots(choice_ids, expert_count):
    flat_ids = choice_ids.reshape(-1).astype(jnp.int32)
    onehot = (flat_ids[:, None] == jnp.arange(expert_count, dtype=jnp.int32)[None, :]).astype(jnp.int32)
    earlier = (jnp.cumsum(onehot, axis=0) - onehot).astype(jnp.int32)
    slot_ids = lax.optimization_barrier(jnp.sum(earlier * onehot, axis=1)).astype(jnp.int32)
    return (flat_ids, slot_ids)

def pair_weights(normed, router_w, choice_ids):
    logits = jnp.dot(normed, router_w, preferred_element_type=jnp.float32)
    picked = jnp.take_along_axis(logits, choice_ids, axis=1)
    first_weight = jax.nn.sigmoid(picked[:, 0] - picked[:, 1])
    return jnp.stack([first_weight, 1.0 - first_weight], axis=1)

def reference(hidden_in, norm_gain, router_w, choices, w_gate, w_up, w_down):
    groups = N_DP * N_EXPERT
    wide_in = hidden_in.astype(jnp.float32)
    normed = (wide_in * lax.rsqrt(lax.optimization_barrier(jnp.mean(wide_in * wide_in, axis=1, keepdims=True)) + eps_norm) * norm_gain).astype(jnp.bfloat16)
    weights = pair_weights(normed, router_w, choices)
    grouped_ids = choices.reshape(groups, TOK_DEV, 2)
    flat_ids, slot_ids = jax.vmap(lambda block_ids: pair_slots(block_ids, E))(grouped_ids)
    group_ids = jnp.arange(groups, dtype=jnp.int32)[:, None]
    row_index = ((group_ids * E + flat_ids) * CAP + slot_ids).astype(jnp.int32).reshape(-1)
    sources = jnp.repeat(normed.reshape(groups, TOK_DEV, D), 2, axis=1).reshape(-1, D)
    buffer = jnp.zeros((groups * E * CAP, D), jnp.bfloat16).at[row_index].set(sources)
    per_expert = buffer.reshape(groups, E, CAP, D).transpose(1, 0, 2, 3).reshape(E, groups * CAP, D)

    def run_expert(operands):
        expert_rows, gate_w, up_w, down_w = operands
        gate_proj = jnp.dot(expert_rows, gate_w, preferred_element_type=jnp.float32)
        up_proj = jnp.dot(expert_rows, up_w, preferred_element_type=jnp.float32)
        hidden = (jax.nn.silu(gate_proj) * up_proj).astype(jnp.bfloat16)
        shares = hidden.reshape(expert_rows.shape[0], N_MP, FF // N_MP).astype(jnp.float32)
        down_parts = down_w.reshape(N_MP, FF // N_MP, D).astype(jnp.float32)
        partial_value = jnp.einsum('rsf,sfd->rsd', shares, down_parts).astype(jnp.bfloat16)
        return lax.optimization_barrier(jnp.sum(partial_value.astype(jnp.float32), axis=1))
    results = lax.map(run_expert, (per_expert, w_gate, w_up, w_down))
    returned = results.reshape(E, groups, CAP, D).transpose(1, 0, 2, 3).reshape(-1, D)
    picked = returned[row_index].reshape(TOKENS, 2, D)
    mixture = lax.optimization_barrier(jnp.sum(picked * weights[:, :, None], axis=1))
    return (wide_in + mixture).astype(jnp.bfloat16)
```

```python
import functools

import jax
import jax.numpy as jnp
from jax import lax
from jax.experimental import pallas as pl
from jax.experimental.pallas import tpu as pltpu
from jax.sharding import PartitionSpec as P

eps_norm = 1e-06
MESH = pl.DeviceIdType.MESH
LANES = 128
TILE = 256
ROWS = 64
f32 = jnp.float32
bf16 = jnp.bfloat16


def xor(a, b, size):
    out, bit = 0, 1
    while bit < size:
        out = out + ((a // bit + b // bit) % 2) * bit
        bit *= 2
    return out


def kernel(
    E, MP, CAP,
    x_ref, gain_ref, router_ref, ch_ref, cht_ref, wg_hbm, wu_hbm, wd_hbm,
    out_ref,
    normed, disp, arr, hid, y, ret, comb, part, zrecv, wg, wu, wd,
    wsem, fs, fr, rs, rr, zs, zr, ls, lr,
):
    T, D = x_ref.shape
    F = wg.shape[1]
    W = D // MP
    HALF = CAP // 2
    far = E - 1
    me = lax.axis_index("expert")
    z = lax.axis_index("mp")
    half = z % 2
    zp = z + 1 - 2 * half

    loads = [
        pltpu.make_async_copy(wg_hbm.at[0], wg, wsem.at[0]),
        pltpu.make_async_copy(wu_hbm.at[0], wu, wsem.at[1]),
        pltpu.make_async_copy(wd_hbm.at[0], wd, wsem.at[2]),
    ]
    for load in loads:
        load.start()

    barrier = pltpu.get_barrier_semaphore()
    for k in range(1, E):
        pl.semaphore_signal(barrier, inc=1, device_id={"expert": xor(me, k, E)}, device_id_type=MESH)
    for d in range(1, MP):
        pl.semaphore_signal(barrier, inc=1, device_id={"mp": (z + d) % MP}, device_id_type=MESH)

    def norm_rows(i, carry):
        rows = pl.ds(pl.multiple_of(i * ROWS, ROWS), ROWS)
        wide = x_ref[rows, :].astype(f32)
        scale = lax.rsqrt(jnp.mean(wide * wide, axis=1, keepdims=True) + eps_norm)
        normed[rows, :] = (wide * scale * gain_ref[...]).astype(bf16)
        return carry

    lax.fori_loop(0, T // ROWS, norm_rows, 0)

    lane = lax.broadcasted_iota(jnp.int32, (T, LANES), 1)
    sub = lax.broadcasted_iota(jnp.int32, (E, T), 0)
    lane_e = jnp.full((T, LANES), -1, jnp.int32)
    sub_e = jnp.full((E, T), -1, jnp.int32)
    for k in range(E):
        lane_e = jnp.where(lane == k, xor(me, k, E), lane_e)
        sub_e = jnp.where(sub == k, xor(me, k, E), sub_e)
    c0, c1 = ch_ref[:, 0:1], ch_ref[:, 1:2]
    is0, is1 = lane_e == c0, lane_e == c1
    any_of = jnp.logical_or(is0, is1)
    any_t = jnp.logical_or(sub_e == cht_ref[0:1, :], sub_e == cht_ref[1:2, :])
    row = lax.broadcasted_iota(jnp.int32, (T, T), 0)
    col = lax.broadcasted_iota(jnp.int32, (T, T), 1)
    lower = (col < row).astype(f32).astype(bf16)
    upper = (row < col).astype(f32).astype(bf16)
    pos = jnp.dot(lower, any_of.astype(f32).astype(bf16), preferred_element_type=f32)
    pos = jnp.where(any_of, pos, -1.0).astype(jnp.int32)
    pos_t = jnp.dot(any_t.astype(f32).astype(bf16), upper, preferred_element_type=f32)
    pos_t = jnp.where(any_t, pos_t, -1.0).astype(jnp.int32)

    slot = lax.broadcasted_iota(jnp.int32, (CAP, T), 0)

    def dispatch(k, dst):
        pick = (slot == pos_t[k : k + 1, :]).astype(f32).astype(bf16)
        for n in range(0, D, 512):
            dst[:, n : n + 512] = jnp.dot(
                pick, normed[:, n : n + 512], preferred_element_type=f32
            ).astype(bf16)

    def forward(k):
        return pltpu.make_async_remote_copy(
            src_ref=disp.at[k - 1], dst_ref=arr.at[k],
            send_sem=fs.at[k], recv_sem=fr.at[k],
            device_id={"expert": xor(me, k, E)}, device_id_type=MESH,
        )

    def rows_of(h):
        return pl.ds(pl.multiple_of(h * HALF, HALF), HALF)

    def forward_far():
        return pltpu.make_async_remote_copy(
            src_ref=disp.at[far - 1, rows_of(half)], dst_ref=arr.at[far, rows_of(half)],
            send_sem=fs.at[far], recv_sem=fr.at[far],
            device_id={"expert": xor(me, far, E)}, device_id_type=MESH,
        )

    def relay():
        return pltpu.make_async_remote_copy(
            src_ref=arr.at[far, rows_of(half)], dst_ref=arr.at[far, rows_of(half)],
            send_sem=ls.at[0], recv_sem=lr.at[0],
            device_id={"mp": zp}, device_id_type=MESH,
        )

    def back(k, m):
        return pltpu.make_async_remote_copy(
            src_ref=y.at[k, m], dst_ref=ret.at[k, m],
            send_sem=rs.at[k, m], recv_sem=rr.at[k, m],
            device_id={"expert": xor(me, k, E)}, device_id_type=MESH,
        )

    def across(d):
        m = (z + d) % MP
        return pltpu.make_async_remote_copy(
            src_ref=part.at[m], dst_ref=zrecv.at[d],
            send_sem=zs.at[d], recv_sem=zr.at[d],
            device_id={"mp": m}, device_id_type=MESH,
        )

    dispatch(far, disp.at[far - 1])
    pl.semaphore_wait(barrier, E - 1 + MP - 1)
    forward_far().start()
    for k in range(1, far):
        dispatch(k, disp.at[k - 1])
        forward(k).start()
    dispatch(0, arr.at[0])

    logits = jnp.dot(normed[...], router_ref[...], preferred_element_type=f32)
    l0 = jnp.sum(jnp.where(lane == c0, logits, 0.0), axis=1, keepdims=True)
    l1 = jnp.sum(jnp.where(lane == c1, logits, 0.0), axis=1, keepdims=True)
    first = jax.nn.sigmoid(l0 - l1)
    place = lax.broadcasted_iota(jnp.int32, (T, CAP), 1)
    for k in range(E):
        e = xor(me, k, E)
        weight = jnp.where(c0 == e, first, 1.0 - first)
        comb[k] = jnp.where(place == pos[:, k : k + 1], weight, 0.0).astype(bf16)

    for load in loads:
        load.wait()

    def ffn(k):
        def tile(cols):
            rows = arr[k]
            gate = jnp.dot(rows, wg[:, cols], preferred_element_type=f32)
            up = jnp.dot(rows, wu[:, cols], preferred_element_type=f32)
            hid[:, cols] = (gate / (1.0 + jnp.exp(-gate)) * up).astype(bf16)

        def step(i, carry):
            tile(pl.ds(pl.multiple_of(i * TILE, TILE), TILE))
            return carry

        lax.fori_loop(0, F // TILE, step, 0)
        if F % TILE:
            tile(pl.ds(F // TILE * TILE, F % TILE))

        def down(j, carry):
            m = (z + 1 + j) % MP
            cols = pl.ds(pl.multiple_of(m * W, W), W)
            y[k, m] = jnp.dot(hid[...], wd[:, cols], preferred_element_type=f32).astype(bf16)

            @pl.when(k > 0)
            def _():
                back(k, m).start()

            return carry

        lax.fori_loop(0, MP, down, 0)

    def block(k, carry):
        @pl.when(jnp.logical_and(k > 0, k < far))
        def _():
            forward(k).wait_recv()

        @pl.when(k == far)
        def _():
            relay().wait_recv()

        ffn(k)

        @pl.when(k == 0)
        def _():
            forward_far().wait_recv()
            relay().start()

        return carry

    lax.fori_loop(0, E, block, 0)

    def mix(m):
        total = jnp.dot(comb[0], y[0, m], preferred_element_type=f32)
        for k in range(1, E):
            back(k, m).wait_recv()
            total = total + jnp.dot(comb[k], ret[k, m], preferred_element_type=f32)
        return total

    def send_chunk(j, carry):
        m = (z + 1 + j) % MP
        part[m] = mix(m).astype(bf16)
        across(1 + j).start()
        return carry

    lax.fori_loop(0, MP - 1, send_chunk, 0)
    cols = pl.ds(pl.multiple_of(z * W, W), W)
    total = x_ref[:, cols].astype(f32) + mix(z)
    for d in range(1, MP):
        across(d).wait_recv()
        total = total + zrecv[d].astype(f32)
    out_ref[...] = total.astype(bf16)

    for k in range(1, far):
        forward(k).wait_send()
    forward_far().wait_send()
    relay().wait_send()

    def drain(k, carry):
        def one(m, c):
            back(k, m).wait_send()
            return c

        return lax.fori_loop(0, MP, one, carry)

    lax.fori_loop(1, E, drain, 0)
    for d in range(1, MP):
        across(d).wait_send()


def per_device(hidden_in, norm_gain, router_w, choices, w_gate, w_up, w_down):
    E = lax.axis_size("expert")
    MP = lax.axis_size("mp")
    T, D = hidden_in.shape
    F = w_gate.shape[2]
    CAP = 3 * T // E
    W = D // MP
    router = jnp.pad(router_w, ((0, 0), (0, LANES - router_w.shape[1])))
    vmem = pl.BlockSpec(memory_space=pltpu.VMEM)
    hbm = pl.BlockSpec(memory_space=pl.ANY)
    dma = pltpu.SemaphoreType.DMA
    rows = E * CAP
    return pl.pallas_call(
        functools.partial(kernel, E, MP, CAP),
        out_shape=jax.ShapeDtypeStruct((T, W), bf16),
        in_specs=[vmem] * 5 + [hbm] * 3,
        out_specs=vmem,
        scratch_shapes=[
            pltpu.VMEM((T, D), bf16),
            pltpu.VMEM((E - 1, CAP, D), bf16),
            pltpu.VMEM((E, CAP, D), bf16),
            pltpu.VMEM((CAP, F), bf16),
            pltpu.VMEM((E, MP, CAP, W), bf16),
            pltpu.VMEM((E, MP, CAP, W), bf16),
            pltpu.VMEM((E, T, CAP), bf16),
            pltpu.VMEM((MP, T, W), bf16),
            pltpu.VMEM((MP, T, W), bf16),
            pltpu.VMEM((D, F), bf16),
            pltpu.VMEM((D, F), bf16),
            pltpu.VMEM((F, D), bf16),
            dma((3,)), dma((E,)), dma((E,)), dma((E, MP)), dma((E, MP)),
            dma((MP,)), dma((MP,)), dma((1,)), dma((1,)),
        ],
        compiler_params=pltpu.CompilerParams(
            collective_id=0, has_side_effects=True, vmem_limit_bytes=62 * 1024 * 1024
        ),
        cost_estimate=pl.CostEstimate(
            flops=6 * rows * D * F, bytes_accessed=6 * D * F, transcendentals=rows * F
        ),
    )(
        hidden_in, norm_gain.reshape(1, D), router, choices, choices.T, w_gate, w_up, w_down
    )


def solution(mesh):
    placed = (
        P(("dp", "expert"), None),
        P(),
        P(),
        P(("dp", "expert"), None),
        P("expert", None, "mp"),
        P("expert", None, "mp"),
        P("expert", "mp", None),
    )
    return jax.shard_map(
        per_device, mesh=mesh, in_specs=placed, out_specs=P(("dp", "expert"), "mp"), check_vma=False
    )
```

```python
import functools

import jax
import jax.numpy as jnp
from jax import lax
from jax.experimental import pallas as pl
from jax.experimental.pallas import tpu as pltpu
from jax.sharding import PartitionSpec as P

eps_norm = 1e-06
MESH = pl.DeviceIdType.MESH
TILE = 256
ROWS = 64
f32 = jnp.float32
bf16 = jnp.bfloat16


def xor(a, b, size):
    out, bit = 0, 1
    while bit < size:
        out = out + ((a // bit + b // bit) % 2) * bit
        bit *= 2
    return out


def kernel(
    E, MP, CAP,
    x_ref, gain_ref, router_ref, ch_ref, wg_hbm, wu_hbm, wd_hbm,
    out_ref,
    normed, disp, arr, hid, y, ret, comb, part, zrecv, zy, wg, wu, wd,
    wsem, fs, fr, rs, rr, zs, zr, ls, lr, ps, pr,
):
    T, D = x_ref.shape
    F = wg.shape[1]
    W = D // MP
    HALF = CAP // 2
    far = E - 1
    me = lax.axis_index("expert")
    z = lax.axis_index("mp")
    half = z % 2
    zp = z + 1 - 2 * half

    loads = [
        pltpu.make_async_copy(wg_hbm.at[0], wg, wsem.at[0]),
        pltpu.make_async_copy(wu_hbm.at[0], wu, wsem.at[1]),
        pltpu.make_async_copy(wd_hbm.at[0], wd, wsem.at[2]),
    ]
    for load in loads:
        load.start()

    barrier = pltpu.get_barrier_semaphore()
    for k in range(1, E):
        pl.semaphore_signal(barrier, inc=1, device_id={"expert": xor(me, k, E)}, device_id_type=MESH)
    for d in range(1, MP):
        pl.semaphore_signal(barrier, inc=1, device_id={"mp": (z + d) % MP}, device_id_type=MESH)

    def norm_rows(i, carry):
        rows = pl.ds(pl.multiple_of(i * ROWS, ROWS), ROWS)
        wide = x_ref[rows, :].astype(f32)
        scale = lax.rsqrt(jnp.mean(wide * wide, axis=1, keepdims=True) + eps_norm)
        normed[rows, :] = (wide * scale * gain_ref[...]).astype(bf16)
        return carry

    lax.fori_loop(0, T // ROWS, norm_rows, 0)

    sub = lax.broadcasted_iota(jnp.int32, (E, T), 0)
    sub_e = jnp.full((E, T), -1, jnp.int32)
    for k in range(E):
        sub_e = jnp.where(sub == k, xor(me, k, E), sub_e)
    c0, c1 = ch_ref[0:1, :], ch_ref[1:2, :]

    def ones(mask):
        return jnp.where(mask, 1.0, 0.0).astype(bf16)

    first_t, any_t = ones(sub_e == c0), ones(jnp.logical_or(sub_e == c0, sub_e == c1))
    row = lax.broadcasted_iota(jnp.int32, (T, T), 0)
    col = lax.broadcasted_iota(jnp.int32, (T, T), 1)
    upper = ones(row < col)
    pos_t = jnp.dot(any_t, upper, preferred_element_type=f32)
    pos_t = jnp.where(any_t > 0, pos_t, -1.0).astype(jnp.int32)

    slot = lax.broadcasted_iota(jnp.int32, (CAP, T), 0)

    def dispatch(k, dst):
        pick = (slot == pos_t[k : k + 1, :]).astype(f32).astype(bf16)
        for n in range(0, D, 512):
            dst[:, n : n + 512] = jnp.dot(
                pick, normed[:, n : n + 512], preferred_element_type=f32
            ).astype(bf16)

    def forward(k):
        return pltpu.make_async_remote_copy(
            src_ref=disp.at[k - 1], dst_ref=arr.at[k],
            send_sem=fs.at[k], recv_sem=fr.at[k],
            device_id={"expert": xor(me, k, E)}, device_id_type=MESH,
        )

    def rows_of(h):
        return pl.ds(pl.multiple_of(h * HALF, HALF), HALF)

    def forward_far():
        return pltpu.make_async_remote_copy(
            src_ref=disp.at[far - 1, rows_of(half)], dst_ref=arr.at[far, rows_of(half)],
            send_sem=fs.at[far], recv_sem=fr.at[far],
            device_id={"expert": xor(me, far, E)}, device_id_type=MESH,
        )

    def relay():
        return pltpu.make_async_remote_copy(
            src_ref=arr.at[far, rows_of(half)], dst_ref=arr.at[far, rows_of(half)],
            send_sem=ls.at[0], recv_sem=lr.at[0],
            device_id={"mp": zp}, device_id_type=MESH,
        )

    def back(k, m):
        return pltpu.make_async_remote_copy(
            src_ref=y.at[k, m], dst_ref=ret.at[k, m],
            send_sem=rs.at[k, m], recv_sem=rr.at[k, m],
            device_id={"expert": xor(me, k, E)}, device_id_type=MESH,
        )

    def back_far(m):
        return pltpu.make_async_remote_copy(
            src_ref=y.at[far, m, rows_of(half)], dst_ref=ret.at[far, m, rows_of(half)],
            send_sem=rs.at[far, m], recv_sem=rr.at[far, m],
            device_id={"expert": xor(me, far, E)}, device_id_type=MESH,
        )

    def swap(m):
        return pltpu.make_async_remote_copy(
            src_ref=y.at[far, m, rows_of(1 - half)], dst_ref=zy.at[m],
            send_sem=ps.at[m], recv_sem=pr.at[m],
            device_id={"mp": zp}, device_id_type=MESH,
        )

    def pair_sum(m):
        swap(m).wait_recv()
        mine = y[far, m, rows_of(half), :].astype(f32)
        y[far, m, rows_of(half), :] = (mine + zy[m].astype(f32)).astype(bf16)
        back_far(m).start()

    def chunk(j):
        other = (2 * (z // 2) + 2 + j) % MP
        late = j // (MP - 2)
        last = j // (MP - 1)
        return other * (1 - late) + (zp * (1 - last) + z * last) * late

    def across(m):
        d = (m - z + MP) % MP
        return pltpu.make_async_remote_copy(
            src_ref=part.at[m], dst_ref=zrecv.at[d],
            send_sem=zs.at[d], recv_sem=zr.at[d],
            device_id={"mp": m}, device_id_type=MESH,
        )

    dispatch(far, disp.at[far - 1])
    pl.semaphore_wait(barrier, E - 1 + MP - 1)
    forward_far().start()
    for k in range(1, far):
        dispatch(k, disp.at[k - 1])
    dispatch(0, arr.at[0])

    def column(left, right):
        return lax.dot_general(
            left, right, (((1,), (1,)), ((), ())), preferred_element_type=f32
        )

    eye = ones(row == col)
    sub_id = lax.broadcasted_iota(jnp.int32, (E, T), 0)
    logits = column(normed[...], router_ref[...])
    l0 = jnp.sum(logits * column(eye, ones(sub_id == c0)), axis=1, keepdims=True)
    l1 = jnp.sum(logits * column(eye, ones(sub_id == c1)), axis=1, keepdims=True)
    first = jax.nn.sigmoid(l0 - l1)
    any_of, first_of = column(eye, any_t), column(eye, first_t)
    pos = column(ones(col < row), any_t)
    pos = jnp.where(any_of > 0.5, pos, -1.0).astype(jnp.int32)
    weight = jnp.where(first_of > 0.5, first, 1.0 - first)
    place = lax.broadcasted_iota(jnp.int32, (T, CAP), 1)
    for k in range(E):
        comb[k] = jnp.where(place == pos[:, k : k + 1], weight[:, k : k + 1], 0.0).astype(bf16)
    empty = jnp.zeros((HALF, W), bf16)
    for m in range(MP):
        ret[far, m, rows_of(1 - half), :] = empty

    forward_far().wait_send()
    for k in range(1, far):
        forward(k).start()
    for load in loads:
        load.wait()

    def hidden(k):
        def tile(cols):
            rows = arr[k]
            gate = jnp.dot(rows, wg[:, cols], preferred_element_type=f32)
            up = jnp.dot(rows, wu[:, cols], preferred_element_type=f32)
            hid[:, cols] = (gate / (1.0 + jnp.exp(-gate)) * up).astype(bf16)

        def step(i, carry):
            tile(pl.ds(pl.multiple_of(i * TILE, TILE), TILE))
            return carry

        lax.fori_loop(0, F // TILE, step, 0)
        if F % TILE:
            tile(pl.ds(F // TILE * TILE, F % TILE))

    def down(k, after):
        def step(j, carry):
            m = chunk(j)
            cols = pl.ds(pl.multiple_of(m * W, W), W)
            y[k, m] = jnp.dot(hid[...], wd[:, cols], preferred_element_type=f32).astype(bf16)
            after(m)
            return carry

        lax.fori_loop(0, MP, step, 0)

    hidden(0)
    down(0, lambda m: None)
    forward_far().wait_recv()
    relay().start()
    relay().wait_recv()
    hidden(far)
    down(far, lambda m: swap(m).start())

    def near(k, carry):
        forward(k).wait_recv()
        hidden(k)

        def after(m):
            back(k, m).start()

            @pl.when(k == 1)
            def _():
                pair_sum(m)

        down(k, after)
        return carry

    lax.fori_loop(1, far, near, 0)

    def mix(m):
        total = jnp.dot(comb[0], y[0, m], preferred_element_type=f32)
        for k in range(1, E):
            if k == far:
                back_far(m).wait_recv()
            else:
                back(k, m).wait_recv()
            total = total + jnp.dot(comb[k], ret[k, m], preferred_element_type=f32)
        return total

    def send_chunk(j, carry):
        m = chunk(j)
        part[m] = mix(m).astype(bf16)
        across(m).start()
        return carry

    lax.fori_loop(0, MP - 1, send_chunk, 0)
    cols = pl.ds(pl.multiple_of(z * W, W), W)
    total = x_ref[:, cols].astype(f32) + mix(z)
    for d in range(1, MP):
        across((z + d) % MP).wait_recv()
        total = total + zrecv[d].astype(f32)
    out_ref[...] = total.astype(bf16)

    for k in range(1, far):
        forward(k).wait_send()
    relay().wait_send()

    def drain(m, carry):
        for k in range(1, far):
            back(k, m).wait_send()
        back_far(m).wait_send()
        swap(m).wait_send()
        return carry

    lax.fori_loop(0, MP, drain, 0)
    for d in range(1, MP):
        across((z + d) % MP).wait_send()


def per_device(hidden_in, norm_gain, router_w, choices, w_gate, w_up, w_down):
    E = lax.axis_size("expert")
    MP = lax.axis_size("mp")
    T, D = hidden_in.shape
    F = w_gate.shape[2]
    CAP = 3 * T // E
    W = D // MP
    vmem = pl.BlockSpec(memory_space=pltpu.VMEM)
    hbm = pl.BlockSpec(memory_space=pl.ANY)
    dma = pltpu.SemaphoreType.DMA
    rows = E * CAP
    return pl.pallas_call(
        functools.partial(kernel, E, MP, CAP),
        out_shape=jax.ShapeDtypeStruct((T, W), bf16),
        in_specs=[vmem] * 4 + [hbm] * 3,
        out_specs=vmem,
        scratch_shapes=[
            pltpu.VMEM((T, D), bf16),
            pltpu.VMEM((E - 1, CAP, D), bf16),
            pltpu.VMEM((E, CAP, D), bf16),
            pltpu.VMEM((CAP, F), bf16),
            pltpu.VMEM((E, MP, CAP, W), bf16),
            pltpu.VMEM((E, MP, CAP, W), bf16),
            pltpu.VMEM((E, T, CAP), bf16),
            pltpu.VMEM((MP, T, W), bf16),
            pltpu.VMEM((MP, T, W), bf16),
            pltpu.VMEM((MP, CAP // 2, W), bf16),
            pltpu.VMEM((D, F), bf16),
            pltpu.VMEM((D, F), bf16),
            pltpu.VMEM((F, D), bf16),
            dma((3,)), dma((E,)), dma((E,)), dma((E, MP)), dma((E, MP)),
            dma((MP,)), dma((MP,)), dma((1,)), dma((1,)), dma((MP,)), dma((MP,)),
        ],
        compiler_params=pltpu.CompilerParams(
            collective_id=0, has_side_effects=True, vmem_limit_bytes=62 * 1024 * 1024
        ),
        cost_estimate=pl.CostEstimate(
            flops=6 * rows * D * F, bytes_accessed=6 * D * F, transcendentals=rows * F
        ),
    )(
        hidden_in, norm_gain.reshape(1, D), router_w.T, choices.T, w_gate, w_up, w_down
    )


def solution(mesh):
    placed = (
        P(("dp", "expert"), None),
        P(),
        P(),
        P(("dp", "expert"), None),
        P("expert", None, "mp"),
        P("expert", None, "mp"),
        P("expert", "mp", None),
    )
    return jax.shard_map(
        per_device, mesh=mesh, in_specs=placed, out_specs=P(("dp", "expert"), "mp"), check_vma=False
    )
```

```python
import functools

import jax
import jax.numpy as jnp
from jax import lax
from jax.experimental import pallas as pl
from jax.experimental.pallas import tpu as pltpu
from jax.sharding import PartitionSpec as P

eps_norm = 1e-06
MESH = pl.DeviceIdType.MESH
TILE = 256
ROWS = 64
GROUP = 4
f32 = jnp.float32
bf16 = jnp.bfloat16


def xor(a, b, size):
    out, bit = 0, 1
    while bit < size:
        out = out + ((a // bit + b // bit) % 2) * bit
        bit *= 2
    return out


def kernel(
    E, MP, CAP,
    x_ref, gain_ref, router_ref, ch_ref, wg_hbm, wu_hbm, wd_hbm,
    out_ref,
    normed, disp, arr, arr_near, hid, y, y_near, ret, comb, part, zrecv, zy, wg, wu, wd,
    wsem, fs, fr, rs, rr, zs, zr, ls, lr, ps, pr,
):
    T, D = x_ref.shape
    F = wg.shape[1]
    W = D // MP
    HALF = CAP // 2
    far = E - 1
    me = lax.axis_index("expert")
    z = lax.axis_index("mp")
    half = z % 2
    zp = z + 1 - 2 * half
    mine = z % GROUP
    QUARTER = CAP // GROUP

    loads = [
        pltpu.make_async_copy(wg_hbm.at[0], wg, wsem.at[0]),
        pltpu.make_async_copy(wu_hbm.at[0], wu, wsem.at[1]),
        pltpu.make_async_copy(wd_hbm.at[0], wd, wsem.at[2]),
    ]
    for load in loads:
        load.start()

    barrier = pltpu.get_barrier_semaphore()
    for k in range(1, E):
        pl.semaphore_signal(barrier, inc=1, device_id={"expert": xor(me, k, E)}, device_id_type=MESH)
    for d in range(1, MP):
        pl.semaphore_signal(barrier, inc=1, device_id={"mp": (z + d) % MP}, device_id_type=MESH)

    def norm_rows(i, carry):
        rows = pl.ds(pl.multiple_of(i * ROWS, ROWS), ROWS)
        wide = x_ref[rows, :].astype(f32)
        scale = lax.rsqrt(jnp.mean(wide * wide, axis=1, keepdims=True) + eps_norm)
        normed[rows, :] = (wide * scale * gain_ref[...]).astype(bf16)
        return carry

    lax.fori_loop(0, T // ROWS, norm_rows, 0)

    sub = lax.broadcasted_iota(jnp.int32, (E, T), 0)
    sub_e = jnp.full((E, T), -1, jnp.int32)
    for k in range(E):
        sub_e = jnp.where(sub == k, xor(me, k, E), sub_e)
    c0, c1 = ch_ref[0:1, :], ch_ref[1:2, :]

    def ones(mask):
        return jnp.where(mask, 1.0, 0.0).astype(bf16)

    first_t, any_t = ones(sub_e == c0), ones(jnp.logical_or(sub_e == c0, sub_e == c1))
    row = lax.broadcasted_iota(jnp.int32, (T, T), 0)
    col = lax.broadcasted_iota(jnp.int32, (T, T), 1)
    upper = ones(row < col)
    pos_t = jnp.dot(any_t, upper, preferred_element_type=f32)
    pos_t = jnp.where(any_t > 0, pos_t, -1.0).astype(jnp.int32)

    slot = lax.broadcasted_iota(jnp.int32, (CAP, T), 0)

    def dispatch(k, dst):
        pick = (slot == pos_t[k : k + 1, :]).astype(f32).astype(bf16)
        for n in range(0, D, 512):
            dst[:, n : n + 512] = jnp.dot(
                pick, normed[:, n : n + 512], preferred_element_type=f32
            ).astype(bf16)

    def near_rows(k):
        return pl.ds((k - 1) * HALF, HALF)

    def forward(k, h):
        return pltpu.make_async_remote_copy(
            src_ref=disp.at[k - 1, pl.ds(h * HALF, HALF)],
            dst_ref=arr_near.at[h, near_rows(k)],
            send_sem=fs.at[k, h], recv_sem=fr.at[k, h],
            device_id={"expert": xor(me, k, E)}, device_id_type=MESH,
        )

    def rows_of(h):
        return pl.ds(pl.multiple_of(h * HALF, HALF), HALF)

    own_quarter = pl.ds(pl.multiple_of(mine * QUARTER, QUARTER), QUARTER)

    def forward_far():
        return pltpu.make_async_remote_copy(
            src_ref=disp.at[far - 1, own_quarter], dst_ref=arr.at[1, own_quarter],
            send_sem=fs.at[far, 0], recv_sem=fr.at[far, 0],
            device_id={"expert": xor(me, far, E)}, device_id_type=MESH,
        )

    def relay(d):
        return pltpu.make_async_remote_copy(
            src_ref=arr.at[1, own_quarter], dst_ref=arr.at[1, own_quarter],
            send_sem=ls.at[d], recv_sem=lr.at[d],
            device_id={"mp": z - mine + (mine + d) % GROUP}, device_id_type=MESH,
        )

    def back(k, h, m):
        return pltpu.make_async_remote_copy(
            src_ref=y_near.at[h, m, near_rows(k)],
            dst_ref=ret.at[k, m, pl.ds(h * HALF, HALF)],
            send_sem=rs.at[k, h, m], recv_sem=rr.at[k, h, m],
            device_id={"expert": xor(me, k, E)}, device_id_type=MESH,
        )

    def back_far(m):
        return pltpu.make_async_remote_copy(
            src_ref=y.at[1, m, rows_of(half)], dst_ref=ret.at[far, m, rows_of(half)],
            send_sem=rs.at[far, 0, m], recv_sem=rr.at[far, 0, m],
            device_id={"expert": xor(me, far, E)}, device_id_type=MESH,
        )

    def swap(m):
        return pltpu.make_async_remote_copy(
            src_ref=y.at[1, m, rows_of(1 - half)], dst_ref=zy.at[m],
            send_sem=ps.at[m], recv_sem=pr.at[m],
            device_id={"mp": zp}, device_id_type=MESH,
        )

    def pair_sum(m):
        swap(m).wait_recv()
        kept = y[1, m, rows_of(half), :].astype(f32)
        y[1, m, rows_of(half), :] = (kept + zy[m].astype(f32)).astype(bf16)
        back_far(m).start()

    def chunk(j):
        other = (2 * (z // 2) + 2 + j) % MP
        late = j // (MP - 2)
        last = j // (MP - 1)
        return other * (1 - late) + (zp * (1 - last) + z * last) * late

    def across(m):
        d = (m - z + MP) % MP
        return pltpu.make_async_remote_copy(
            src_ref=part.at[m], dst_ref=zrecv.at[d],
            send_sem=zs.at[d], recv_sem=zr.at[d],
            device_id={"mp": m}, device_id_type=MESH,
        )

    dispatch(far, disp.at[far - 1])
    pl.semaphore_wait(barrier, E - 1 + MP - 1)
    forward_far().start()
    for k in range(1, far):
        dispatch(k, disp.at[k - 1])
    dispatch(0, arr.at[0])

    def column(left, right):
        return lax.dot_general(
            left, right, (((1,), (1,)), ((), ())), preferred_element_type=f32
        )

    eye = ones(row == col)
    sub_id = lax.broadcasted_iota(jnp.int32, (E, T), 0)
    logits = column(normed[...], router_ref[...])
    l0 = jnp.sum(logits * column(eye, ones(sub_id == c0)), axis=1, keepdims=True)
    l1 = jnp.sum(logits * column(eye, ones(sub_id == c1)), axis=1, keepdims=True)
    first = jax.nn.sigmoid(l0 - l1)
    any_of, first_of = column(eye, any_t), column(eye, first_t)
    pos = column(ones(col < row), any_t)
    pos = jnp.where(any_of > 0.5, pos, -1.0).astype(jnp.int32)
    weight = jnp.where(first_of > 0.5, first, 1.0 - first)
    place = lax.broadcasted_iota(jnp.int32, (T, CAP), 1)
    for k in range(E):
        comb[k] = jnp.where(place == pos[:, k : k + 1], weight[:, k : k + 1], 0.0).astype(bf16)
    empty = jnp.zeros((HALF, W), bf16)
    for m in range(MP):
        ret[far, m, rows_of(1 - half), :] = empty

    forward_far().wait_send()
    for k in range(1, far):
        forward(k, 0).start()
    forward_far().wait_recv()
    for d in range(1, GROUP):
        relay(d).start()
    for load in loads:
        load.wait()

    def hidden(source):
        def tile(cols):
            rows = source[...]
            gate = jnp.dot(rows, wg[:, cols], preferred_element_type=f32)
            up = jnp.dot(rows, wu[:, cols], preferred_element_type=f32)
            hid[: rows.shape[0], cols] = (gate / (1.0 + jnp.exp(-gate)) * up).astype(bf16)

        def step(i, carry):
            tile(pl.ds(pl.multiple_of(i * TILE, TILE), TILE))
            return carry

        lax.fori_loop(0, F // TILE, step, 0)
        if F % TILE:
            tile(pl.ds(F // TILE * TILE, F % TILE))

    def down(count, target, after):
        def step(j, carry):
            m = chunk(j)
            cols = pl.ds(pl.multiple_of(m * W, W), W)
            target[m] = jnp.dot(
                hid[:count, :], wd[:, cols], preferred_element_type=f32
            ).astype(bf16)
            after(m)
            return carry

        lax.fori_loop(0, MP, step, 0)

    def near(h, also):
        def after(m):
            for k in range(1, far):
                back(k, h, m).start()
            also(m)

        hidden(arr_near.at[h])
        down((E - 2) * HALF, y_near.at[h], after)

    hidden(arr.at[0])
    down(CAP, y.at[0], lambda m: None)
    for k in range(1, far):
        forward(k, 0).wait_send()
        forward(k, 1).start()
    for k in range(1, far):
        forward(k, 0).wait_recv()
    near(0, lambda m: None)
    for d in range(1, GROUP):
        relay(d).wait_recv()
    hidden(arr.at[1])
    down(CAP, y.at[1], lambda m: swap(m).start())
    for k in range(1, far):
        forward(k, 1).wait_recv()
    near(1, pair_sum)

    def mix(m):
        total = jnp.dot(comb[0], y[0, m], preferred_element_type=f32)
        for k in range(1, E):
            if k == far:
                back_far(m).wait_recv()
            else:
                back(k, 0, m).wait_recv()
                back(k, 1, m).wait_recv()
            total = total + jnp.dot(comb[k], ret[k, m], preferred_element_type=f32)
        return total

    def send_chunk(j, carry):
        m = chunk(j)
        part[m] = mix(m).astype(bf16)
        across(m).start()
        return carry

    lax.fori_loop(0, MP - 1, send_chunk, 0)
    cols = pl.ds(pl.multiple_of(z * W, W), W)
    total = x_ref[:, cols].astype(f32) + mix(z)
    for d in range(1, MP):
        across((z + d) % MP).wait_recv()
        total = total + zrecv[d].astype(f32)
    out_ref[...] = total.astype(bf16)

    for k in range(1, far):
        forward(k, 1).wait_send()
    for d in range(1, GROUP):
        relay(d).wait_send()

    def drain(m, carry):
        for k in range(1, far):
            back(k, 0, m).wait_send()
            back(k, 1, m).wait_send()
        back_far(m).wait_send()
        swap(m).wait_send()
        return carry

    lax.fori_loop(0, MP, drain, 0)
    for d in range(1, MP):
        across((z + d) % MP).wait_send()


def per_device(hidden_in, norm_gain, router_w, choices, w_gate, w_up, w_down):
    E = lax.axis_size("expert")
    MP = lax.axis_size("mp")
    T, D = hidden_in.shape
    F = w_gate.shape[2]
    CAP = 3 * T // E
    W = D // MP
    vmem = pl.BlockSpec(memory_space=pltpu.VMEM)
    hbm = pl.BlockSpec(memory_space=pl.ANY)
    dma = pltpu.SemaphoreType.DMA
    rows = E * CAP
    near_count = (E - 2) * CAP // 2
    return pl.pallas_call(
        functools.partial(kernel, E, MP, CAP),
        out_shape=jax.ShapeDtypeStruct((T, W), bf16),
        in_specs=[vmem] * 4 + [hbm] * 3,
        out_specs=vmem,
        scratch_shapes=[
            pltpu.VMEM((T, D), bf16),
            pltpu.VMEM((E - 1, CAP, D), bf16),
            pltpu.VMEM((2, CAP, D), bf16),
            pltpu.VMEM((2, near_count, D), bf16),
            pltpu.VMEM((max(CAP, near_count), F), bf16),
            pltpu.VMEM((2, MP, CAP, W), bf16),
            pltpu.VMEM((2, MP, near_count, W), bf16),
            pltpu.VMEM((E, MP, CAP, W), bf16),
            pltpu.VMEM((E, T, CAP), bf16),
            pltpu.VMEM((MP, T, W), bf16),
            pltpu.VMEM((MP, T, W), bf16),
            pltpu.VMEM((MP, CAP // 2, W), bf16),
            pltpu.VMEM((D, F), bf16),
            pltpu.VMEM((D, F), bf16),
            pltpu.VMEM((F, D), bf16),
            dma((3,)), dma((E, 2)), dma((E, 2)), dma((E, 2, MP)), dma((E, 2, MP)),
            dma((MP,)), dma((MP,)), dma((GROUP,)), dma((GROUP,)), dma((MP,)), dma((MP,)),
        ],
        compiler_params=pltpu.CompilerParams(
            collective_id=0, has_side_effects=True, vmem_limit_bytes=62 * 1024 * 1024
        ),
        cost_estimate=pl.CostEstimate(
            flops=6 * rows * D * F, bytes_accessed=6 * D * F, transcendentals=rows * F
        ),
    )(
        hidden_in, norm_gain.reshape(1, D), router_w.T, choices.T, w_gate, w_up, w_down
    )


def solution(mesh):
    placed = (
        P(("dp", "expert"), None),
        P(),
        P(),
        P(("dp", "expert"), None),
        P("expert", None, "mp"),
        P("expert", None, "mp"),
        P("expert", "mp", None),
    )
    return jax.shard_map(
        per_device, mesh=mesh, in_specs=placed, out_specs=P(("dp", "expert"), "mp"), check_vma=False
    )
```

```python
import functools

import jax
import jax.numpy as jnp
from jax import lax
from jax.experimental import pallas as pl
from jax.experimental.pallas import tpu as pltpu
from jax.sharding import PartitionSpec as P

eps_norm = 1e-06
MESH = pl.DeviceIdType.MESH
TILE = 256
ROWS = 64
GROUP = 4
f32 = jnp.float32
bf16 = jnp.bfloat16


def xor(a, b, size):
    out, bit = 0, 1
    while bit < size:
        out = out + ((a // bit + b // bit) % 2) * bit
        bit *= 2
    return out


def kernel(
    E, MP, CAP,
    x_ref, gain_ref, router_ref, ch_ref, wg_hbm, wu_hbm, wd_hbm,
    out_ref,
    normed, disp, arr, arr_near, hid, y, y_near, ret, comb, part, zrecv, zy, wg, wu, wd,
    wsem, fs, fr, rs, rr, zs, zr, ls, lr, ps, pr,
):
    T, D = x_ref.shape
    F = wg.shape[1]
    W = D // MP
    HALF = CAP // 2
    far = E - 1
    me = lax.axis_index("expert")
    z = lax.axis_index("mp")
    half = z % 2
    zp = z + 1 - 2 * half
    mine = z % GROUP
    QUARTER = CAP // GROUP

    loads = [
        pltpu.make_async_copy(wg_hbm.at[0], wg, wsem.at[0]),
        pltpu.make_async_copy(wu_hbm.at[0], wu, wsem.at[1]),
        pltpu.make_async_copy(wd_hbm.at[0], wd, wsem.at[2]),
    ]
    for load in loads:
        load.start()

    barrier = pltpu.get_barrier_semaphore()
    for k in range(1, E):
        pl.semaphore_signal(barrier, inc=1, device_id={"expert": xor(me, k, E)}, device_id_type=MESH)
    for d in range(1, MP):
        pl.semaphore_signal(barrier, inc=1, device_id={"mp": (z + d) % MP}, device_id_type=MESH)

    def norm_rows(i, carry):
        rows = pl.ds(pl.multiple_of(i * ROWS, ROWS), ROWS)
        wide = x_ref[rows, :].astype(f32)
        scale = lax.rsqrt(jnp.mean(wide * wide, axis=1, keepdims=True) + eps_norm)
        normed[rows, :] = (wide * scale * gain_ref[...]).astype(bf16)
        return carry

    lax.fori_loop(0, T // ROWS, norm_rows, 0)

    sub = lax.broadcasted_iota(jnp.int32, (E, T), 0)
    sub_e = jnp.full((E, T), -1, jnp.int32)
    for k in range(E):
        sub_e = jnp.where(sub == k, xor(me, k, E), sub_e)
    c0, c1 = ch_ref[0:1, :], ch_ref[1:2, :]

    def ones(mask):
        return jnp.where(mask, 1.0, 0.0).astype(bf16)

    first_t, any_t = ones(sub_e == c0), ones(jnp.logical_or(sub_e == c0, sub_e == c1))
    row = lax.broadcasted_iota(jnp.int32, (T, T), 0)
    col = lax.broadcasted_iota(jnp.int32, (T, T), 1)
    upper = ones(row < col)
    pos_t = jnp.dot(any_t, upper, preferred_element_type=f32)
    pos_t = jnp.where(any_t > 0, pos_t, -1.0).astype(jnp.int32)

    def dispatch(k, dst, begin, count):
        slot = begin + lax.broadcasted_iota(jnp.int32, (count, T), 0)
        pick = ones(slot == pos_t[k : k + 1, :])
        for n in range(0, D, 512):
            dst[:, n : n + 512] = jnp.dot(
                pick, normed[:, n : n + 512], preferred_element_type=f32
            ).astype(bf16)

    def near_rows(k):
        return pl.ds((k - 1) * HALF, HALF)

    def forward(k, h):
        return pltpu.make_async_remote_copy(
            src_ref=disp.at[k - 1, pl.ds(h * HALF, HALF)],
            dst_ref=arr_near.at[h, near_rows(k)],
            send_sem=fs.at[k, h], recv_sem=fr.at[k, h],
            device_id={"expert": xor(me, k, E)}, device_id_type=MESH,
        )

    def rows_of(h):
        return pl.ds(pl.multiple_of(h * HALF, HALF), HALF)

    own_quarter = pl.ds(pl.multiple_of(mine * QUARTER, QUARTER), QUARTER)

    def forward_far():
        return pltpu.make_async_remote_copy(
            src_ref=disp.at[far - 1, own_quarter], dst_ref=arr.at[1, own_quarter],
            send_sem=fs.at[far, 0], recv_sem=fr.at[far, 0],
            device_id={"expert": xor(me, far, E)}, device_id_type=MESH,
        )

    def relay(d):
        return pltpu.make_async_remote_copy(
            src_ref=arr.at[1, own_quarter], dst_ref=arr.at[1, own_quarter],
            send_sem=ls.at[d], recv_sem=lr.at[d],
            device_id={"mp": z - mine + (mine + d) % GROUP}, device_id_type=MESH,
        )

    def back(k, h, m):
        return pltpu.make_async_remote_copy(
            src_ref=y_near.at[h, m, near_rows(k)],
            dst_ref=ret.at[k, m, pl.ds(h * HALF, HALF)],
            send_sem=rs.at[k, h, m], recv_sem=rr.at[k, h, m],
            device_id={"expert": xor(me, k, E)}, device_id_type=MESH,
        )

    def back_far(m):
        return pltpu.make_async_remote_copy(
            src_ref=y.at[1, m, rows_of(half)], dst_ref=ret.at[far, m, rows_of(half)],
            send_sem=rs.at[far, 0, m], recv_sem=rr.at[far, 0, m],
            device_id={"expert": xor(me, far, E)}, device_id_type=MESH,
        )

    def swap(m):
        return pltpu.make_async_remote_copy(
            src_ref=y.at[1, m, rows_of(1 - half)], dst_ref=zy.at[m],
            send_sem=ps.at[m], recv_sem=pr.at[m],
            device_id={"mp": zp}, device_id_type=MESH,
        )

    def pair_sum(m):
        swap(m).wait_recv()
        kept = y[1, m, rows_of(half), :].astype(f32)
        y[1, m, rows_of(half), :] = (kept + zy[m].astype(f32)).astype(bf16)
        back_far(m).start()

    def chunk(j):
        return (zp * (1 - j % 2) + z * (j % 2) + 2 * (j // 2 + 1)) % MP

    def far_chunk(j):
        return (2 * (z // 2) + 2 + j) % MP

    def across(j):
        return pltpu.make_async_remote_copy(
            src_ref=part.at[j], dst_ref=zrecv.at[j],
            send_sem=zs.at[j], recv_sem=zr.at[j],
            device_id={"mp": zp * (1 - j % 2) + chunk(j) * (j % 2)}, device_id_type=MESH,
        )

    dispatch(far, disp.at[far - 1, own_quarter], mine * QUARTER, QUARTER)
    pl.semaphore_wait(barrier, E - 1 + MP - 1)
    forward_far().start()
    for k in range(1, far):
        dispatch(k, disp.at[k - 1, pl.ds(0, HALF)], 0, HALF)
    dispatch(0, arr.at[0], 0, CAP)
    forward_far().wait_send()
    for k in range(1, far):
        forward(k, 0).start()
    forward_far().wait_recv()
    for d in range(1, GROUP):
        relay(d).start()
    for k in range(1, far):
        dispatch(k, disp.at[k - 1, pl.ds(HALF, HALF)], HALF, HALF)

    def column(left, right):
        return lax.dot_general(
            left, right, (((1,), (1,)), ((), ())), preferred_element_type=f32
        )

    eye = ones(row == col)
    sub_id = lax.broadcasted_iota(jnp.int32, (E, T), 0)
    logits = column(normed[...], router_ref[...])
    l0 = jnp.sum(logits * column(eye, ones(sub_id == c0)), axis=1, keepdims=True)
    l1 = jnp.sum(logits * column(eye, ones(sub_id == c1)), axis=1, keepdims=True)
    first = jax.nn.sigmoid(l0 - l1)
    any_of, first_of = column(eye, any_t), column(eye, first_t)
    pos = column(ones(col < row), any_t)
    pos = jnp.where(any_of > 0.5, pos, -1.0).astype(jnp.int32)
    weight = jnp.where(first_of > 0.5, first, 1.0 - first)
    place = lax.broadcasted_iota(jnp.int32, (T, CAP), 1)
    for k in range(E):
        comb[k] = jnp.where(place == pos[:, k : k + 1], weight[:, k : k + 1], 0.0).astype(bf16)
    empty = jnp.zeros((HALF, W), bf16)
    for m in range(MP):
        ret[far, m, rows_of(1 - half), :] = empty

    for load in loads:
        load.wait()

    def hidden(source, also=None):
        def tile(cols):
            rows = source[...]
            gate = jnp.dot(rows, wg[:, cols], preferred_element_type=f32)
            up = jnp.dot(rows, wu[:, cols], preferred_element_type=f32)
            hid[: rows.shape[0], cols] = (gate / (1.0 + jnp.exp(-gate)) * up).astype(bf16)

        def step(i, carry):
            tile(pl.ds(pl.multiple_of(i * TILE, TILE), TILE))
            if also is not None:
                pl.when(i == F // TILE // 2)(also)
            return carry

        lax.fori_loop(0, F // TILE, step, 0)
        if F % TILE:
            tile(pl.ds(F // TILE * TILE, F % TILE))

    def down(count, target, order, after):
        def step(j, carry):
            m = order(j)
            cols = pl.ds(pl.multiple_of(m * W, W), W)
            target[m] = jnp.dot(
                hid[:count, :], wd[:, cols], preferred_element_type=f32
            ).astype(bf16)
            after(j, m)
            return carry

        lax.fori_loop(0, MP, step, 0)

    def near(h, between, also):
        def after(j, m):
            for k in range(1, far):
                back(k, h, m).start()
            also(j)

        between(lambda during: hidden(arr_near.at[h], during))
        down((E - 2) * HALF, y_near.at[h], chunk, after)

    hidden(arr.at[0])
    down(CAP, y.at[0], chunk, lambda j, m: None)
    for k in range(1, far):
        forward(k, 0).wait_send()
        forward(k, 1).start()
    for k in range(1, far):
        forward(k, 0).wait_recv()
    near(0, lambda work: work(None), lambda j: None)
    for d in range(1, GROUP):
        relay(d).wait_recv()
    hidden(arr.at[1])
    down(CAP, y.at[1], far_chunk, lambda j, m: swap(m).start())
    for k in range(1, far):
        forward(k, 1).wait_recv()

    def first_sums(work):
        work(lambda: pair_sum(far_chunk(0)))
        pair_sum(far_chunk(1))

    def later_sums(j):
        @pl.when(j > 1)
        def _():
            pair_sum(far_chunk(j))

    near(1, first_sums, later_sums)

    def mix(m):
        total = jnp.dot(comb[0], y[0, m], preferred_element_type=f32)
        for k in range(1, E):
            if k == far:
                back_far(m).wait_recv()
            else:
                back(k, 0, m).wait_recv()
                back(k, 1, m).wait_recv()
            total = total + jnp.dot(comb[k], ret[k, m], preferred_element_type=f32)
        return total

    def send_chunks(i, carry):
        even, odd = 2 * i, 2 * i + 1
        part[even] = mix(chunk(even)).astype(bf16)
        across(even).start()
        total = mix(chunk(odd))
        across(even).wait_recv()
        part[odd] = (total + zrecv[even].astype(f32)).astype(bf16)
        across(odd).start()
        return carry

    lax.fori_loop(0, MP // 2 - 1, send_chunks, 0)
    part[MP - 2] = mix(zp).astype(bf16)
    across(MP - 2).start()
    cols = pl.ds(pl.multiple_of(z * W, W), W)
    total = x_ref[:, cols].astype(f32) + mix(z)
    across(MP - 2).wait_recv()
    total = total + zrecv[MP - 2].astype(f32)
    for j in range(1, MP - 2, 2):
        across(j).wait_recv()
        total = total + zrecv[j].astype(f32)
    out_ref[...] = total.astype(bf16)

    for k in range(1, far):
        forward(k, 1).wait_send()
    for d in range(1, GROUP):
        relay(d).wait_send()

    def drain(m, carry):
        for k in range(1, far):
            back(k, 0, m).wait_send()
            back(k, 1, m).wait_send()
        back_far(m).wait_send()
        swap(m).wait_send()
        return carry

    lax.fori_loop(0, MP, drain, 0)
    for j in range(MP - 1):
        across(j).wait_send()


def per_device(hidden_in, norm_gain, router_w, choices, w_gate, w_up, w_down):
    E = lax.axis_size("expert")
    MP = lax.axis_size("mp")
    T, D = hidden_in.shape
    F = w_gate.shape[2]
    CAP = 3 * T // E
    W = D // MP
    vmem = pl.BlockSpec(memory_space=pltpu.VMEM)
    hbm = pl.BlockSpec(memory_space=pl.ANY)
    dma = pltpu.SemaphoreType.DMA
    rows = E * CAP
    near_count = (E - 2) * CAP // 2
    return pl.pallas_call(
        functools.partial(kernel, E, MP, CAP),
        out_shape=jax.ShapeDtypeStruct((T, W), bf16),
        in_specs=[vmem] * 4 + [hbm] * 3,
        out_specs=vmem,
        scratch_shapes=[
            pltpu.VMEM((T, D), bf16),
            pltpu.VMEM((E - 1, CAP, D), bf16),
            pltpu.VMEM((2, CAP, D), bf16),
            pltpu.VMEM((2, near_count, D), bf16),
            pltpu.VMEM((max(CAP, near_count), F), bf16),
            pltpu.VMEM((2, MP, CAP, W), bf16),
            pltpu.VMEM((2, MP, near_count, W), bf16),
            pltpu.VMEM((E, MP, CAP, W), bf16),
            pltpu.VMEM((E, T, CAP), bf16),
            pltpu.VMEM((MP, T, W), bf16),
            pltpu.VMEM((MP, T, W), bf16),
            pltpu.VMEM((MP, CAP // 2, W), bf16),
            pltpu.VMEM((D, F), bf16),
            pltpu.VMEM((D, F), bf16),
            pltpu.VMEM((F, D), bf16),
            dma((3,)), dma((E, 2)), dma((E, 2)), dma((E, 2, MP)), dma((E, 2, MP)),
            dma((MP,)), dma((MP,)), dma((GROUP,)), dma((GROUP,)), dma((MP,)), dma((MP,)),
        ],
        compiler_params=pltpu.CompilerParams(
            collective_id=0, has_side_effects=True, vmem_limit_bytes=62 * 1024 * 1024
        ),
        cost_estimate=pl.CostEstimate(
            flops=6 * rows * D * F, bytes_accessed=6 * D * F, transcendentals=rows * F
        ),
    )(
        hidden_in, norm_gain.reshape(1, D), router_w.T, choices.T, w_gate, w_up, w_down
    )


def solution(mesh):
    placed = (
        P(("dp", "expert"), None),
        P(),
        P(),
        P(("dp", "expert"), None),
        P("expert", None, "mp"),
        P("expert", None, "mp"),
        P("expert", "mp", None),
    )
    return jax.shard_map(
        per_device, mesh=mesh, in_specs=placed, out_specs=P(("dp", "expert"), "mp"), check_vma=False
    )
```

```python
import functools

import jax
import jax.numpy as jnp
from jax import lax
from jax.experimental import pallas as pl
from jax.experimental.pallas import tpu as pltpu
from jax.sharding import PartitionSpec as P

eps_norm = 1e-06
MESH = pl.DeviceIdType.MESH
TILE = 256
ROWS = 64
GROUP = 4
f32 = jnp.float32
bf16 = jnp.bfloat16


def xor(a, b, size):
    out, bit = 0, 1
    while bit < size:
        out = out + ((a // bit + b // bit) % 2) * bit
        bit *= 2
    return out


def kernel(
    E, MP, CAP,
    x_ref, gain_ref, router_ref, ch_ref, wg_hbm, wu_hbm, wd_hbm,
    out_ref,
    normed, disp, arr, arr_near, hid, y, y_near, ret, comb, part, zrecv, zy, wg, wu, wd,
    wsem, fs, fr, rs, rr, zs, zr, ls, lr, ps, pr, ns, nr,
):
    T, D = x_ref.shape
    F = wg.shape[1]
    W = D // MP
    HALF = CAP // 2
    far = E - 1
    me = lax.axis_index("expert")
    z = lax.axis_index("mp")
    half = z % 2
    zp = z + 1 - 2 * half
    mine = z % GROUP
    QUARTER = CAP // GROUP

    loads = [
        pltpu.make_async_copy(wg_hbm.at[0], wg, wsem.at[0]),
        pltpu.make_async_copy(wu_hbm.at[0], wu, wsem.at[1]),
        pltpu.make_async_copy(wd_hbm.at[0], wd, wsem.at[2]),
    ]
    for load in loads:
        load.start()

    barrier = pltpu.get_barrier_semaphore()
    for k in range(1, E):
        pl.semaphore_signal(barrier, inc=1, device_id={"expert": xor(me, k, E)}, device_id_type=MESH)
    for d in range(1, MP):
        pl.semaphore_signal(barrier, inc=1, device_id={"mp": (z + d) % MP}, device_id_type=MESH)

    def norm_rows(i, carry):
        rows = pl.ds(pl.multiple_of(i * ROWS, ROWS), ROWS)
        wide = x_ref[rows, :].astype(f32)
        scale = lax.rsqrt(jnp.mean(wide * wide, axis=1, keepdims=True) + eps_norm)
        normed[rows, :] = (wide * scale * gain_ref[...]).astype(bf16)
        return carry

    lax.fori_loop(0, T // ROWS, norm_rows, 0)

    sub = lax.broadcasted_iota(jnp.int32, (E, T), 0)
    sub_e = jnp.full((E, T), -1, jnp.int32)
    for k in range(E):
        sub_e = jnp.where(sub == k, xor(me, k, E), sub_e)
    c0, c1 = ch_ref[0:1, :], ch_ref[1:2, :]

    def ones(mask):
        return jnp.where(mask, 1.0, 0.0).astype(bf16)

    first_t, any_t = ones(sub_e == c0), ones(jnp.logical_or(sub_e == c0, sub_e == c1))
    row = lax.broadcasted_iota(jnp.int32, (T, T), 0)
    col = lax.broadcasted_iota(jnp.int32, (T, T), 1)
    upper = ones(row < col)
    pos_t = jnp.dot(any_t, upper, preferred_element_type=f32)
    pos_t = jnp.where(any_t > 0, pos_t, -1.0).astype(jnp.int32)

    def dispatch(k, dst, begin, count):
        slot = begin + lax.broadcasted_iota(jnp.int32, (count, T), 0)
        pick = ones(slot == pos_t[k : k + 1, :])
        for n in range(0, D, 512):
            dst[:, n : n + 512] = jnp.dot(
                pick, normed[:, n : n + 512], preferred_element_type=f32
            ).astype(bf16)

    def near_rows(k):
        return pl.ds((k - 1) * HALF, HALF)

    def late_rows(base):
        return pl.ds(pl.multiple_of(base + half * QUARTER, QUARTER), QUARTER)

    def forward(k):
        return pltpu.make_async_remote_copy(
            src_ref=disp.at[k - 1, pl.ds(0, HALF)],
            dst_ref=arr_near.at[0, near_rows(k)],
            send_sem=fs.at[k, 0], recv_sem=fr.at[k, 0],
            device_id={"expert": xor(me, k, E)}, device_id_type=MESH,
        )

    def forward_late(k):
        return pltpu.make_async_remote_copy(
            src_ref=disp.at[k - 1, late_rows(HALF)],
            dst_ref=arr_near.at[1, late_rows((k - 1) * HALF)],
            send_sem=fs.at[k, 1], recv_sem=fr.at[k, 1],
            device_id={"expert": xor(me, k, E)}, device_id_type=MESH,
        )

    def relay_late(k):
        return pltpu.make_async_remote_copy(
            src_ref=arr_near.at[1, late_rows((k - 1) * HALF)],
            dst_ref=arr_near.at[1, late_rows((k - 1) * HALF)],
            send_sem=ns.at[k], recv_sem=nr.at[k],
            device_id={"mp": zp}, device_id_type=MESH,
        )

    def rows_of(h):
        return pl.ds(pl.multiple_of(h * HALF, HALF), HALF)

    own_quarter = pl.ds(pl.multiple_of(mine * QUARTER, QUARTER), QUARTER)

    def forward_far():
        return pltpu.make_async_remote_copy(
            src_ref=disp.at[far - 1, own_quarter], dst_ref=arr.at[1, own_quarter],
            send_sem=fs.at[far, 0], recv_sem=fr.at[far, 0],
            device_id={"expert": xor(me, far, E)}, device_id_type=MESH,
        )

    def relay(d):
        return pltpu.make_async_remote_copy(
            src_ref=arr.at[1, own_quarter], dst_ref=arr.at[1, own_quarter],
            send_sem=ls.at[d], recv_sem=lr.at[d],
            device_id={"mp": z - mine + (mine + d) % GROUP}, device_id_type=MESH,
        )

    def back(k, h, m):
        return pltpu.make_async_remote_copy(
            src_ref=y_near.at[h, m, near_rows(k)],
            dst_ref=ret.at[k, m, pl.ds(h * HALF, HALF)],
            send_sem=rs.at[k, h, m], recv_sem=rr.at[k, h, m],
            device_id={"expert": xor(me, k, E)}, device_id_type=MESH,
        )

    def back_far(m):
        return pltpu.make_async_remote_copy(
            src_ref=y.at[1, m, rows_of(half)], dst_ref=ret.at[far, m, rows_of(half)],
            send_sem=rs.at[far, 0, m], recv_sem=rr.at[far, 0, m],
            device_id={"expert": xor(me, far, E)}, device_id_type=MESH,
        )

    def swap(m):
        return pltpu.make_async_remote_copy(
            src_ref=y.at[1, m, rows_of(1 - half)], dst_ref=zy.at[m],
            send_sem=ps.at[m], recv_sem=pr.at[m],
            device_id={"mp": zp}, device_id_type=MESH,
        )

    def pair_sum(m):
        swap(m).wait_recv()
        kept = y[1, m, rows_of(half), :].astype(f32)
        y[1, m, rows_of(half), :] = (kept + zy[m].astype(f32)).astype(bf16)
        back_far(m).start()

    def chunk(j):
        return (zp * (1 - j % 2) + z * (j % 2) + 2 * (j // 2 + 1)) % MP

    def far_chunk(j):
        return (2 * (z // 2) + 2 + j) % MP

    def across(j):
        return pltpu.make_async_remote_copy(
            src_ref=part.at[j], dst_ref=zrecv.at[j],
            send_sem=zs.at[j], recv_sem=zr.at[j],
            device_id={"mp": zp * (1 - j % 2) + chunk(j) * (j % 2)}, device_id_type=MESH,
        )

    dispatch(far, disp.at[far - 1, own_quarter], mine * QUARTER, QUARTER)
    pl.semaphore_wait(barrier, E - 1 + MP - 1)
    forward_far().start()
    for k in range(1, far):
        dispatch(k, disp.at[k - 1, pl.ds(0, HALF)], 0, HALF)
    dispatch(0, arr.at[0], 0, CAP)
    forward_far().wait_send()
    for k in range(1, far):
        forward(k).start()
    forward_far().wait_recv()
    for d in range(1, GROUP):
        relay(d).start()
    for k in range(1, far):
        dispatch(k, disp.at[k - 1, late_rows(HALF)], HALF + half * QUARTER, QUARTER)

    def column(left, right):
        return lax.dot_general(
            left, right, (((1,), (1,)), ((), ())), preferred_element_type=f32
        )

    eye = ones(row == col)
    sub_id = lax.broadcasted_iota(jnp.int32, (E, T), 0)
    logits = column(normed[...], router_ref[...])
    l0 = jnp.sum(logits * column(eye, ones(sub_id == c0)), axis=1, keepdims=True)
    l1 = jnp.sum(logits * column(eye, ones(sub_id == c1)), axis=1, keepdims=True)
    first = jax.nn.sigmoid(l0 - l1)
    any_of, first_of = column(eye, any_t), column(eye, first_t)
    pos = column(ones(col < row), any_t)
    pos = jnp.where(any_of > 0.5, pos, -1.0).astype(jnp.int32)
    weight = jnp.where(first_of > 0.5, first, 1.0 - first)
    place = lax.broadcasted_iota(jnp.int32, (T, CAP), 1)
    for k in range(E):
        comb[k] = jnp.where(place == pos[:, k : k + 1], weight[:, k : k + 1], 0.0).astype(bf16)
    empty = jnp.zeros((HALF, W), bf16)
    for m in range(MP):
        ret[far, m, rows_of(1 - half), :] = empty

    for load in loads:
        load.wait()

    def hidden(source, also=None):
        def tile(cols):
            rows = source[...]
            gate = jnp.dot(rows, wg[:, cols], preferred_element_type=f32)
            up = jnp.dot(rows, wu[:, cols], preferred_element_type=f32)
            hid[: rows.shape[0], cols] = (gate / (1.0 + jnp.exp(-gate)) * up).astype(bf16)

        def step(i, carry):
            tile(pl.ds(pl.multiple_of(i * TILE, TILE), TILE))
            if also is not None:
                pl.when(i == F // TILE // 2)(also)
            return carry

        lax.fori_loop(0, F // TILE, step, 0)
        if F % TILE:
            tile(pl.ds(F // TILE * TILE, F % TILE))

    def down(count, target, order, after):
        def step(j, carry):
            m = order(j)
            cols = pl.ds(pl.multiple_of(m * W, W), W)
            target[m] = jnp.dot(
                hid[:count, :], wd[:, cols], preferred_element_type=f32
            ).astype(bf16)
            after(j, m)
            return carry

        lax.fori_loop(0, MP, step, 0)

    def near(h, between, also):
        def after(j, m):
            for k in range(1, far):
                back(k, h, m).start()
            also(j)

        between(lambda during: hidden(arr_near.at[h], during))
        down((E - 2) * HALF, y_near.at[h], chunk, after)

    hidden(arr.at[0])
    down(CAP, y.at[0], chunk, lambda j, m: None)
    for k in range(1, far):
        forward(k).wait_send()
        forward_late(k).start()
    for k in range(1, far):
        forward(k).wait_recv()

    def pass_late(work):
        work(None)
        for k in range(1, far):
            forward_late(k).wait_recv()
            relay_late(k).start()

    near(0, pass_late, lambda j: None)
    for d in range(1, GROUP):
        relay(d).wait_recv()
    hidden(arr.at[1])
    down(CAP, y.at[1], far_chunk, lambda j, m: swap(m).start())
    for k in range(1, far):
        relay_late(k).wait_recv()

    def first_sums(work):
        work(lambda: pair_sum(far_chunk(0)))
        pair_sum(far_chunk(1))

    def later_sums(j):
        @pl.when(j > 1)
        def _():
            pair_sum(far_chunk(j))

    near(1, first_sums, later_sums)

    def mix(m):
        total = jnp.dot(comb[0], y[0, m], preferred_element_type=f32)
        for k in range(1, E):
            if k == far:
                back_far(m).wait_recv()
            else:
                back(k, 0, m).wait_recv()
                back(k, 1, m).wait_recv()
            total = total + jnp.dot(comb[k], ret[k, m], preferred_element_type=f32)
        return total

    def send_chunks(i, carry):
        even, odd = 2 * i, 2 * i + 1
        part[even] = mix(chunk(even)).astype(bf16)
        across(even).start()
        total = mix(chunk(odd))
        across(even).wait_recv()
        part[odd] = (total + zrecv[even].astype(f32)).astype(bf16)
        across(odd).start()
        return carry

    lax.fori_loop(0, MP // 2 - 1, send_chunks, 0)
    part[MP - 2] = mix(zp).astype(bf16)
    across(MP - 2).start()
    cols = pl.ds(pl.multiple_of(z * W, W), W)
    total = x_ref[:, cols].astype(f32) + mix(z)
    across(MP - 2).wait_recv()
    total = total + zrecv[MP - 2].astype(f32)
    for j in range(1, MP - 2, 2):
        across(j).wait_recv()
        total = total + zrecv[j].astype(f32)
    out_ref[...] = total.astype(bf16)

    for k in range(1, far):
        forward_late(k).wait_send()
        relay_late(k).wait_send()
    for d in range(1, GROUP):
        relay(d).wait_send()

    def drain(m, carry):
        for k in range(1, far):
            back(k, 0, m).wait_send()
            back(k, 1, m).wait_send()
        back_far(m).wait_send()
        swap(m).wait_send()
        return carry

    lax.fori_loop(0, MP, drain, 0)
    for j in range(MP - 1):
        across(j).wait_send()


def per_device(hidden_in, norm_gain, router_w, choices, w_gate, w_up, w_down):
    E = lax.axis_size("expert")
    MP = lax.axis_size("mp")
    T, D = hidden_in.shape
    F = w_gate.shape[2]
    CAP = 3 * T // E
    W = D // MP
    vmem = pl.BlockSpec(memory_space=pltpu.VMEM)
    hbm = pl.BlockSpec(memory_space=pl.ANY)
    dma = pltpu.SemaphoreType.DMA
    rows = E * CAP
    near_count = (E - 2) * CAP // 2
    return pl.pallas_call(
        functools.partial(kernel, E, MP, CAP),
        out_shape=jax.ShapeDtypeStruct((T, W), bf16),
        in_specs=[vmem] * 4 + [hbm] * 3,
        out_specs=vmem,
        scratch_shapes=[
            pltpu.VMEM((T, D), bf16),
            pltpu.VMEM((E - 1, CAP, D), bf16),
            pltpu.VMEM((2, CAP, D), bf16),
            pltpu.VMEM((2, near_count, D), bf16),
            pltpu.VMEM((max(CAP, near_count), F), bf16),
            pltpu.VMEM((2, MP, CAP, W), bf16),
            pltpu.VMEM((2, MP, near_count, W), bf16),
            pltpu.VMEM((E, MP, CAP, W), bf16),
            pltpu.VMEM((E, T, CAP), bf16),
            pltpu.VMEM((MP, T, W), bf16),
            pltpu.VMEM((MP, T, W), bf16),
            pltpu.VMEM((MP, CAP // 2, W), bf16),
            pltpu.VMEM((D, F), bf16),
            pltpu.VMEM((D, F), bf16),
            pltpu.VMEM((F, D), bf16),
            dma((3,)), dma((E, 2)), dma((E, 2)), dma((E, 2, MP)), dma((E, 2, MP)),
            dma((MP,)), dma((MP,)), dma((GROUP,)), dma((GROUP,)), dma((MP,)), dma((MP,)), dma((E,)), dma((E,)),
        ],
        compiler_params=pltpu.CompilerParams(
            collective_id=0, has_side_effects=True, vmem_limit_bytes=62 * 1024 * 1024
        ),
        cost_estimate=pl.CostEstimate(
            flops=6 * rows * D * F, bytes_accessed=6 * D * F, transcendentals=rows * F
        ),
    )(
        hidden_in, norm_gain.reshape(1, D), router_w.T, choices.T, w_gate, w_up, w_down
    )


def solution(mesh):
    placed = (
        P(("dp", "expert"), None),
        P(),
        P(),
        P(("dp", "expert"), None),
        P("expert", None, "mp"),
        P("expert", None, "mp"),
        P("expert", "mp", None),
    )
    return jax.shard_map(
        per_device, mesh=mesh, in_specs=placed, out_specs=P(("dp", "expert"), "mp"), check_vma=False
    )
```
